32 devices in a mesh: section: 2 (over core), seq: 16 (over z, y, x).
Axes of the slice: x: 2, y: 2, z: 4, core: 2. Of those that a mesh axis runs over, the one named last changes fastest.
Arguments:
- bases: int32 [2, 8192], P(None, 'seq'), may hold values from 0 to 3
- stem_weight: bfloat16 [15, 4, 1536], replicated, may hold values from -1.5 to 1.5
- gains: bfloat16 [2, 1536], P('section'), may hold values from 0.099609375 to 1.8984375
- depth_taps: bfloat16 [2, 5, 1536], P('section'), may hold values from -2.5 to 2.5
- point_weight: bfloat16 [2, 1536, 1536], P('section', 'seq'), may hold values from -0.15625 to 0.15625
Outputs:
- encoded: bfloat16 [2, 2048, 1536], P(None, 'seq', 'section')
The draws below stay inside these ranges and needn't reach their ends.
All inputs are finite; a program needn't handle non-finite values.
Results may differ from the reference program's by a relative error of at most 0.015.
Values may be sent and summed in bfloat16 or wider, within the bound.
A program may use at most 64 MiB of HBM per device.

```python
import jax
import jax.numpy as jnp
from jax import lax

C = 1536
K0 = 15
KERNEL_TAPS = 5
DILATION_STEP = 2
MB = 2
L0 = 8192
N_SECTION = 2


def place_ends(array, own_key, least, high):
    longest = array.shape.index(max(array.shape))
    spots = []
    for shift in (0, 1):
        where = [jax.random.randint(jax.random.fold_in(own_key, axis), (), 0, length) for axis, length in enumerate(array.shape)]
        where[longest] = (where[longest] + shift) % array.shape[longest]
        spots.append(tuple(where))
    return array.at[spots[0]].set(least).at[spots[1]].set(high)


def block_levels(rng, dims, shards, low, high):
    factor_of = 1.0
    for dim, blocks in shards:
        heights = jax.random.uniform(jax.random.fold_in(jax.random.fold_in(rng, 6), dim), (blocks,), jnp.float32, low / len(shards), high / len(shards))
        factor_of = factor_of * jnp.repeat(jnp.exp(heights), dims[dim] // blocks).reshape((-1,) + (1,) * (len(dims) - 1 - dim))
    return factor_of


def bell_draw(own_key, shape, deviation, limit, cuts=(), kind=jnp.bfloat16):
    values = deviation * jax.random.normal(own_key, shape, jnp.float32)
    if cuts:
        values = values * block_levels(own_key, shape, cuts, -0.22, 0.18)
    return jnp.clip(values, -limit, limit).astype(kind)


def setup_inputs(seed: int = 0) -> dict:
    splits = jax.random.split(jax.random.key(seed), 6)
    bases = place_ends(jax.random.randint(splits[0], (MB, L0), 0, 4), jax.random.fold_in(splits[0], 1), 0, 3).astype(jnp.int32)
    stem_weight = bell_draw(splits[1], (K0, 4, C), K0 ** -0.5, 1.5)
    gains = jnp.clip(1.0 + 0.18 * jax.random.normal(splits[2], (N_SECTION, C), jnp.float32), 0.099609375, 1.8984375).astype(jnp.bfloat16)
    depth_taps = bell_draw(splits[3], (N_SECTION, KERNEL_TAPS, C), KERNEL_TAPS ** -0.5, 2.5, ((0, 2),))
    point_weight = bell_draw(splits[4], (N_SECTION, C, C), C ** -0.5, 0.15625, ((0, 2), (1, 16)))
    return {"bases": bases, "stem_weight": stem_weight, "gains": gains, "depth_taps": depth_taps, "point_weight": point_weight}


def normalize_gelu(rows, gain_row):
    values = rows.astype(jnp.float32)
    square_mean = lax.optimization_barrier(jnp.mean(values * values, axis=-1, keepdims=True))
    scaled = values * lax.rsqrt(square_mean + 1e-06) * gain_row.astype(jnp.float32)
    return jax.nn.gelu(scaled, approximate=True).astype(jnp.bfloat16)

def filter_rows(extended_rows, kernel_weight, length_total):
    summed = jnp.zeros((length_total, extended_rows.shape[1]), jnp.float32)
    for offset_amount in range(kernel_weight.shape[0]):
        window_rows = extended_rows[offset_amount * DILATION_STEP:offset_amount * DILATION_STEP + length_total].astype(jnp.float32)
        summed = summed + kernel_weight[offset_amount].astype(jnp.float32) * window_rows
    return summed.astype(jnp.bfloat16)

def halve_rows(rows):
    return lax.optimization_barrier(jnp.max(rows.reshape(rows.shape[0] // 2, 2, rows.shape[1]), axis=1))

def stem_rows(extended_ids, stem_weight, length_total):
    one_hot = (extended_ids[:, None] == jnp.arange(1, 5, dtype=jnp.int32)[None, :]).astype(jnp.bfloat16)
    window_rows = jnp.concatenate([one_hot[offset_amount:offset_amount + length_total] for offset_amount in range(stem_weight.shape[0])], axis=1)
    flat = stem_weight.reshape(stem_weight.shape[0] * 4, stem_weight.shape[2])
    return jnp.dot(window_rows, flat, preferred_element_type=jnp.float32).astype(jnp.bfloat16)

def encode_one(sequence, stem_weight, gains, depth_taps, point_weight):
    margin = K0 // 2
    extended_ids = jnp.pad(sequence + 1, (margin, margin))
    current = stem_rows(extended_ids, stem_weight, sequence.shape[0])
    spread_width = KERNEL_TAPS // 2 * DILATION_STEP
    for level in range(N_SECTION):
        activated = normalize_gelu(current, gains[level])
        extended_rows = jnp.pad(activated, ((spread_width, spread_width), (0, 0)))
        filtered = filter_rows(extended_rows, depth_taps[level], current.shape[0])
        mixed_rows = (current.astype(jnp.float32) + jnp.dot(filtered, point_weight[level], preferred_element_type=jnp.float32)).astype(jnp.bfloat16)
        current = halve_rows(mixed_rows)
    return current

def reference(bases, stem_weight, gains, depth_taps, point_weight):
    outputs = []
    for sequence_index in range(MB):
        outputs.append(encode_one(bases[sequence_index], stem_weight, gains, depth_taps, point_weight))
    return jnp.stack(outputs)
```

```python
import functools

import jax
import jax.numpy as jnp
from jax import lax
from jax.experimental import pallas as pl
from jax.experimental.pallas import tpu as pltpu
from jax.sharding import PartitionSpec as P

DILATION_STEP = 2


def padded(array, sides, width):
    for axis, dim in sides:
        size, length = (lax.axis_size(axis), array.shape[dim])
        up = [(i, (i + 1) % size) for i in range(size - 1)]
        down = [(j, i) for i, j in up]
        last = lax.slice_in_dim(array, length - width, length, axis=dim)
        first = lax.slice_in_dim(array, 0, width, axis=dim)
        before = lax.ppermute(last, axis, up)
        after = lax.ppermute(first, axis, down)
        array = jnp.concatenate([before, array, after], axis=dim)
    return array


def shortened(array):

    def short(part):
        return part.astype(jnp.bfloat16) if part.dtype == jnp.float32 else part

    return jax.tree.map(short, array)


def passed_along(array, axis, by):
    length = lax.axis_size(axis)
    pairs = [(i, i + by) for i in range(length) if 0 <= i + by < length]
    return lax.ppermute(array, axis, pairs)


def from_root(value, axis, source):
    kept = jnp.where(lax.axis_index(axis) == source, value, 0).astype(value.dtype)
    return lax.psum(kept, axis)


def normalize_gelu(rows, gain_row):
    values = rows.astype(jnp.float32)
    square_mean = jnp.mean(values * values, axis=-1, keepdims=True)
    scaled = values * lax.rsqrt(square_mean + 1e-06) * gain_row.astype(jnp.float32)
    return jax.nn.gelu(scaled, approximate=True).astype(jnp.bfloat16)


def filter_rows(extended_rows, kernel_weight, length_total):
    summed = jnp.zeros((length_total, extended_rows.shape[1]), jnp.float32)
    for offset_amount in range(kernel_weight.shape[0]):
        window_rows = extended_rows[
            offset_amount * DILATION_STEP : offset_amount * DILATION_STEP + length_total
        ].astype(jnp.float32)
        summed = summed + kernel_weight[offset_amount].astype(jnp.float32) * window_rows
    return summed.astype(jnp.bfloat16)


def halve_rows(rows):
    return jnp.max(rows.reshape(rows.shape[0] // 2, 2, rows.shape[1]), axis=1)


def stem_rows(extended_ids, stem_weight, length_total):
    one_hot = (extended_ids[:, None] == jnp.arange(1, 5, dtype=jnp.int32)[None, :]).astype(
        jnp.bfloat16
    )
    window_rows = jnp.concatenate(
        [
            one_hot[offset_amount : offset_amount + length_total]
            for offset_amount in range(stem_weight.shape[0])
        ],
        axis=1,
    )
    flat = stem_weight.reshape(stem_weight.shape[0] * 4, stem_weight.shape[2])
    return jnp.dot(window_rows, flat, preferred_element_type=jnp.float32).astype(jnp.bfloat16)


def shards(bases, stem_weight, gains, depth_taps, point_weight):
    section_count = lax.axis_size("section")
    position = lax.axis_index("section")
    sequences, width_rows = bases.shape
    channels = stem_weight.shape[2]
    margin = stem_weight.shape[0] // 2
    padded_ids = padded(bases + 1, (("seq", 1),), margin)
    stems = jnp.stack(
        [stem_rows(padded_ids[index], stem_weight, width_rows) for index in range(sequences)]
    )
    gain_row = gains[0]
    kernel_weight = depth_taps[0]
    spread_width = kernel_weight.shape[0] // 2 * DILATION_STEP
    half_rows = width_rows // 2
    final_rows = width_rows >> section_count
    steps_total = sequences + section_count - 1
    first_section = position == 0
    valid_count = jnp.right_shift(jnp.int32(width_rows), position)

    def edge_rims(stem_now, inbox):
        head = jnp.where(first_section, stem_now[:spread_width], inbox[:spread_width])
        inbox_tail = lax.dynamic_slice_in_dim(inbox, valid_count - spread_width, spread_width, 0)
        tail = jnp.where(first_section, stem_now[width_rows - spread_width :], inbox_tail)
        edges = jnp.concatenate([head, tail], axis=0)
        framed = padded(normalize_gelu(edges, gain_row), (("seq", 0),), spread_width)
        return (framed[:spread_width], framed[3 * spread_width :])

    def prepare(level_rows, left_rim, right_rim):
        activated = normalize_gelu(level_rows, gain_row)
        extended_rows = jnp.concatenate([left_rim, activated, right_rim], axis=0)
        return filter_rows(extended_rows, kernel_weight, level_rows.shape[0])

    def complete(level_rows, product):
        pooled = halve_rows((level_rows.astype(jnp.float32) + product).astype(jnp.bfloat16))
        if pooled.shape[0] < half_rows:
            pooled = jnp.concatenate(
                [pooled, jnp.zeros((half_rows - pooled.shape[0], channels), jnp.bfloat16)], axis=0
            )
        return pooled

    def pass_on(pooled):
        return jax.tree.map(
            lambda part, own: part.astype(own.dtype),
            passed_along(shortened(pooled), "section", 1),
            pooled,
        )

    inbox_start = jnp.zeros((half_rows, channels), jnp.bfloat16)
    first_rows = stems[0]
    left_first, right_first = edge_rims(first_rows, inbox_start)
    filtered_first = prepare(first_rows, left_first, right_first)
    weights_full = lax.all_gather(point_weight, "seq", axis=1, tiled=True)[0]
    product_first = jnp.dot(filtered_first, weights_full, preferred_element_type=jnp.float32)
    inbox = pass_on(complete(first_rows, product_first))
    outbox = jnp.zeros((sequences, final_rows, channels), jnp.bfloat16)

    def make_level(level):
        count = width_rows >> level

        def run(operands):
            stem_now, inbox_now, left_rim, right_rim = operands
            level_rows = stem_now if level == 0 else inbox_now[:count]
            filtered = prepare(level_rows, left_rim, right_rim)
            product = jnp.dot(filtered, weights_full, preferred_element_type=jnp.float32)
            return complete(level_rows, product)

        return run

    branches = [make_level(level) for level in range(section_count)]

    def advance(inbox_now, outbox_now, step_index):
        micro_index = step_index - position
        live = (micro_index >= 0) & (micro_index < sequences)
        clipped = jnp.clip(micro_index, 0, sequences - 1)
        stem_now = lax.dynamic_index_in_dim(stems, clipped, 0, keepdims=False)
        left_rim, right_rim = edge_rims(stem_now, inbox_now)

        def working(operands):
            return lax.switch(position, branches, operands)

        def resting(operands):
            return jnp.zeros((half_rows, channels), jnp.bfloat16)

        pooled = lax.cond(live, working, resting, (stem_now, inbox_now, left_rim, right_rim))
        keep = live & (position == section_count - 1)
        updated = lax.dynamic_update_index_in_dim(outbox_now, pooled[:final_rows], clipped, 0)
        return (pooled, jnp.where(keep, updated, outbox_now))

    def middle_step(carry, step_index):
        pooled, outbox_next = advance(carry[0], carry[1], step_index)
        return ((pass_on(pooled), outbox_next), None)

    (inbox, outbox), unused = lax.scan(
        middle_step, (inbox, outbox), jnp.arange(1, steps_total - 1, dtype=jnp.int32)
    )
    pooled_last, outbox = advance(inbox, outbox, jnp.int32(steps_total - 1))
    coarsest = from_root(outbox, "section", section_count - 1)
    out_width = channels // section_count
    return lax.dynamic_slice_in_dim(coarsest, position * out_width, out_width, 2)


GROUP = 4
BLOCK = 16
MESH = pl.DeviceIdType.MESH


def gelu_of(scaled):
    inner = scaled * (0.7978845608028654 + 0.03567740813636141 * (scaled * scaled))
    return (0.5 * scaled) * (1.0 + jnp.tanh(inner))


def encoder_kernel(
    n_seq,
    runs,
    taps,
    ids_ref,
    stem_ref,
    params_ref,
    weight_ref,
    out_ref,
    ids_all,
    params_all,
    one_hot,
    window,
    x0_buf,
    act_buf,
    d0_buf,
    x1_buf,
    d1_buf,
    weights,
    send_sem,
    recv_sem,
    side_send,
    side_recv,
    local_sem,
    half_send,
    half_recv,
):
    j = lax.axis_index("section")
    q = lax.axis_index("seq")
    n_z = n_seq // 4
    x, y, z = lax.rem(q, 2), lax.rem(lax.div(q, 2), 2), lax.div(q, 4)
    to_x, to_y = 1 - 2 * x, 2 * (1 - 2 * y)
    to_a = (1 - j) * to_x + j * to_y
    to_b = j * to_x + (1 - j) * to_y
    right, left = lax.rem(q + 1, n_seq), lax.rem(q + n_seq - 1, n_seq)
    other = 1 - j
    depth, width = weight_ref.shape[1], weight_ref.shape[2] // 2
    channels = 2 * width
    rows = x0_buf.shape[1]
    margin = (rows - runs) // 2
    sequences = out_ref.shape[0]

    def at_z(offset):
        return lax.rem(z + offset, n_z) * 4 + lax.rem(q, 4)

    barrier = pltpu.get_barrier_semaphore()
    greeted = [(other, q), (j, q + to_a), (j, q + to_b), (j, left), (j, right)]
    greeted += [(j, at_z(offset)) for offset in range(1, n_z)]
    for device in greeted:
        pl.semaphore_signal(barrier, inc=1, device_id=device, device_id_type=MESH)
    pl.semaphore_wait(barrier, len(greeted))

    def remote(src, dst, send, recv, device):
        return pltpu.make_async_remote_copy(
            src_ref=src,
            dst_ref=dst,
            send_sem=send,
            recv_sem=recv,
            device_id=device,
            device_id_type=MESH,
        )

    def chunk(level, index):
        start = pl.multiple_of(index * depth, BLOCK)
        return weights.at[level, pl.ds(start, depth)]

    def columns(half):
        return pl.ds(pl.multiple_of(half * width, 128), width)

    local = pltpu.make_async_copy(
        weight_ref.at[0, :, columns(j)], chunk(j, q), local_sem.at[0]
    )
    swap = remote(
        weight_ref.at[0, :, columns(other)], chunk(j, q), side_send.at[0], side_recv.at[0], (other, q)
    )
    swapped = remote(
        weight_ref.at[0, :, columns(other)],
        chunk(other, q),
        side_send.at[0],
        side_recv.at[0],
        (other, q),
    )
    swap.start()
    local.start()
    to_right = remote(ids_ref, ids_all.at[0], side_send.at[1], side_recv.at[1], (j, right))
    to_left = remote(ids_ref, ids_all.at[2], side_send.at[2], side_recv.at[2], (j, left))
    to_right.start()
    to_left.start()
    share = remote(params_ref, params_all.at[j], side_send.at[3], side_recv.at[3], (other, q))
    shared = remote(params_ref, params_all.at[other], side_send.at[3], side_recv.at[3], (other, q))
    share.start()
    keep = pltpu.make_async_copy(params_ref, params_all.at[j], local_sem.at[1])
    keep.start()
    keep_ids = pltpu.make_async_copy(ids_ref, ids_all.at[1], local_sem.at[2])
    keep_ids.start()

    def z_copy(level, offset, incoming):
        index = at_z(n_z - offset) if incoming else q
        slot = offset - 1
        part = chunk(level, index)
        return remote(
            part, part, send_sem.at[level, slot], recv_sem.at[level, slot], (j, at_z(offset))
        )

    def a_copy(level, offset, incoming):
        index = at_z(n_z - offset) if offset else q
        slot = n_z - 1 + offset
        part = chunk(level, index + to_a if incoming else index)
        return remote(
            part, part, send_sem.at[level, slot], recv_sem.at[level, slot], (j, q + to_a)
        )

    def b_copy(level, offset, crossed, incoming):
        index = at_z(n_z - offset) if offset else q
        index = index + to_a if crossed else index
        slot = 2 * n_z - 1 + offset + (n_z if crossed else 0)
        part = chunk(level, index + to_b if incoming else index)
        return remote(
            part, part, send_sem.at[level, slot], recv_sem.at[level, slot], (j, q + to_b)
        )

    def own(level):
        for offset in range(1, n_z):
            z_copy(level, offset, False).start()
        a_copy(level, 0, False).start()
        b_copy(level, 0, False, False).start()

    def z_event(level, offset):
        z_copy(level, offset, True).wait_recv()
        a_copy(level, offset, False).start()
        b_copy(level, offset, False, False).start()

    def a_event(level, offset):
        a_copy(level, offset, True).wait_recv()
        b_copy(level, offset, True, False).start()

    def b_events(level):
        for offset in range(n_z):
            b_copy(level, offset, False, True).wait_recv()
        for offset in range(n_z):
            b_copy(level, offset, True, True).wait_recv()

    def sends_done(level):
        for offset in range(1, n_z):
            z_copy(level, offset, False).wait_send()
        for offset in range(n_z):
            a_copy(level, offset, False).wait_send()
            b_copy(level, offset, False, False).wait_send()
            b_copy(level, offset, True, False).wait_send()

    to_right.wait_recv()
    to_left.wait_recv()
    keep_ids.wait()
    here = jnp.concatenate(
        [
            jnp.where(q > 0, ids_all[0], -1),
            ids_all[1],
            jnp.where(q < n_seq - 1, ids_all[2], -1),
        ],
        axis=1,
    )
    lanes = here.shape[1]
    span = one_hot.shape[1]
    four = lax.broadcasted_iota(jnp.int32, (4, span), 0)
    one_hot[...] = jnp.zeros_like(one_hot)
    rolled = {}
    for b in range(sequences):
        for c in range(GROUP):
            for k in range(taps):
                away = c + k - taps // 2
                shift, klass = away // GROUP, b * GROUP + away % GROUP
                if shift not in rolled:
                    begin = runs - margin + shift
                    rolled[shift] = pltpu.roll(here, (lanes - begin) % lanes, 1)
                line = rolled[shift][klass : klass + 1, :span]
                hit = jnp.broadcast_to(line, (4, span)) == four
                one_hot[4 * k : 4 * k + 4, :] = hit.astype(jnp.float32)
            window[b * GROUP + c] = one_hot[...].T[:rows].astype(jnp.bfloat16)

    local.wait()
    swapped.wait_recv()
    own(0)
    own(1)
    keep.wait()
    shared.wait_recv()

    def row_mask(start, total_low, total_high, count):
        index = lax.broadcasted_iota(jnp.int32, (count, 1), 0) + start
        return (index >= total_low) & (index < total_high)

    low = margin - q * runs
    high = low + n_seq * runs
    blocks = rows // BLOCK
    inverse = 1.0 / channels

    def first_block(step, carry):
        stream = lax.div(step, blocks)
        start = pl.multiple_of(lax.rem(step, blocks) * BLOCK, BLOCK)
        part = pl.ds(start, BLOCK)
        found = jnp.dot(
            window[stream, part, :], stem_ref[...], preferred_element_type=jnp.float32
        ).astype(jnp.bfloat16)
        x0_buf[stream, part, :] = found
        values = found.astype(jnp.float32)
        mean = jnp.sum(values * values, axis=1, keepdims=True) * inverse
        scaled = values * lax.rsqrt(mean + 1e-06) * params_all[0, 0:1, :]
        act_buf[stream, part, :] = jnp.where(
            row_mask(start, low, high, BLOCK), gelu_of(scaled), 0.0
        )
        return carry

    col_blocks = channels // 128

    def first_filter(step, carry):
        col = pl.ds(pl.multiple_of(lax.rem(step, col_blocks) * 128, 128), 128)
        pair = lax.div(step, col_blocks)
        even = lax.div(pair, 2) * GROUP + lax.rem(pair, 2)
        odd = even + 2
        tap = [params_all[0, 1 + k : 2 + k, col] for k in range(5)]
        a0, a2 = act_buf[even, :, col], act_buf[odd, :, col]
        a0_before, a2_before = pltpu.roll(a0, 1, 0), pltpu.roll(a2, 1, 0)
        a0_after, a2_after = pltpu.roll(a0, rows - 1, 0), pltpu.roll(a2, rows - 1, 0)
        d0_buf[even, :, col] = (
            tap[0] * a0_before + tap[1] * a2_before + tap[2] * a0 + tap[3] * a2 + tap[4] * a0_after
        ).astype(jnp.bfloat16)
        d0_buf[odd, :, col] = (
            tap[0] * a2_before + tap[1] * a0 + tap[2] * a2 + tap[3] * a0_after + tap[4] * a2_after
        ).astype(jnp.bfloat16)
        return carry

    def interleaved(total, body, events):
        done = 0
        for number, event in enumerate(events):
            until = total * (number + 1) // (len(events) + 1)
            lax.fori_loop(done, until, body, 0)
            event()
            done = until
        lax.fori_loop(done, total, body, 0)

    def later(function, *args):
        return lambda: function(*args)

    z_events = [[later(z_event, level, o) for o in range(1, n_z)] for level in range(2)]
    a_events = [[later(a_event, level, o) for o in range(n_z)] for level in range(2)]

    interleaved(sequences * GROUP * blocks, first_block, z_events[0] + a_events[0])
    interleaved(sequences * 2 * col_blocks, first_filter, z_events[1] + a_events[1])

    def half_copy(stream, incoming):
        part = x1_buf.at[stream, other if incoming else j]
        return remote(part, part, half_send.at[stream], half_recv.at[stream], (other, q))

    b_events(0)
    for stream in range(2 * sequences):
        taken = d0_buf[2 * stream : 2 * stream + 2].reshape(2 * rows, channels)
        product = jnp.dot(taken, weights[0], preferred_element_type=jnp.float32)
        level_rows = x0_buf[2 * stream : 2 * stream + 2, :, columns(j)].reshape(2 * rows, width)
        mixed = (level_rows.astype(jnp.float32) + product).astype(jnp.bfloat16)
        x1_buf[stream, j] = jnp.maximum(mixed[:rows], mixed[rows:])
        half_copy(stream, False).start()

    def second_block(stream):
        def run(step, carry):
            start = pl.multiple_of(step * BLOCK, BLOCK)
            part = pl.ds(start, BLOCK)
            values = jnp.concatenate(
                [x1_buf[stream, 0, part, :], x1_buf[stream, 1, part, :]], axis=1
            ).astype(jnp.float32)
            mean = jnp.sum(values * values, axis=1, keepdims=True) * inverse
            scaled = values * lax.rsqrt(mean + 1e-06) * params_all[1, 0:1, :]
            act_buf[stream, part, :] = jnp.where(
                row_mask(start, low, high, BLOCK), gelu_of(scaled), 0.0
            )
            return carry

        return run

    def second_filter(stream):
        def run(step, carry):
            col = pl.ds(pl.multiple_of(step * 128, 128), 128)
            tap = [params_all[1, 1 + k : 2 + k, col] for k in range(5)]
            a = act_buf[stream, :, col]
            total = tap[2] * a
            for k in (0, 1, 3, 4):
                total = total + tap[k] * pltpu.roll(a, (2 - k) % rows, 0)
            d1_buf[stream, :, col] = total[margin : margin + runs].astype(jnp.bfloat16)
            return carry

        return run

    for stream in range(2 * sequences):
        half_copy(stream, True).wait_recv()
        lax.fori_loop(0, blocks, second_block(stream), 0)
        lax.fori_loop(0, col_blocks, second_filter(stream), 0)

    b_events(1)
    for b in range(sequences):
        taken = d1_buf[2 * b : 2 * b + 2].reshape(2 * runs, channels)
        product = jnp.dot(taken, weights[1], preferred_element_type=jnp.float32)
        level_rows = x1_buf[2 * b : 2 * b + 2, j, margin : margin + runs, :]
        level_rows = level_rows.reshape(2 * runs, width)
        mixed = (level_rows.astype(jnp.float32) + product).astype(jnp.bfloat16)
        out_ref[b] = jnp.maximum(mixed[:runs], mixed[runs:])

    swap.wait_send()
    to_right.wait_send()
    to_left.wait_send()
    share.wait_send()
    for stream in range(2 * sequences):
        half_copy(stream, False).wait_send()
    sends_done(0)
    sends_done(1)


def fused(bases, stem_weight, gains, depth_taps, point_weight):
    n_seq = lax.axis_size("seq")
    sequences, width_rows = bases.shape
    taps, kinds, channels = stem_weight.shape
    runs = width_rows // GROUP
    rows = runs + BLOCK
    streams = sequences * GROUP
    ids = bases.reshape(sequences, runs, GROUP).transpose(0, 2, 1).reshape(streams, runs)
    stem = jnp.pad(stem_weight.reshape(taps * kinds, channels), ((0, 128 - taps * kinds), (0, 0)))
    params = jnp.concatenate([gains, depth_taps[0]], axis=0).astype(jnp.float32)
    params = jnp.pad(params, ((0, 8 - params.shape[0]), (0, 0)))
    half = channels // 2
    n_z = n_seq // 4
    slots = 4 * n_z - 1
    vmem = pl.BlockSpec(memory_space=pltpu.VMEM)
    dma = pltpu.SemaphoreType.DMA
    return pl.pallas_call(
        functools.partial(encoder_kernel, n_seq, runs, taps),
        out_shape=jax.ShapeDtypeStruct((sequences, runs, half), jnp.bfloat16),
        in_specs=[vmem] * 4,
        out_specs=vmem,
        scratch_shapes=[
            pltpu.VMEM((3, streams, runs), jnp.int32),
            pltpu.VMEM((2, 8, channels), jnp.float32),
            pltpu.VMEM((128, 2 * runs), jnp.float32),
            pltpu.VMEM((streams, rows, 128), jnp.bfloat16),
            pltpu.VMEM((streams, rows, channels), jnp.bfloat16),
            pltpu.VMEM((streams, rows, channels), jnp.float32),
            pltpu.VMEM((streams, rows, channels), jnp.bfloat16),
            pltpu.VMEM((streams // 2, 2, rows, half), jnp.bfloat16),
            pltpu.VMEM((streams // 2, runs, channels), jnp.bfloat16),
            pltpu.VMEM((2, channels, half), jnp.bfloat16),
            dma((2, slots)),
            dma((2, slots)),
            dma((4,)),
            dma((4,)),
            dma((3,)),
            dma((streams // 2,)),
            dma((streams // 2,)),
        ],
        compiler_params=pltpu.CompilerParams(
            collective_id=0, has_side_effects=True, vmem_limit_bytes=56 * 1024 * 1024
        ),
    )(ids, stem, params, point_weight)


def chosen(bases, stem_weight, gains, depth_taps, point_weight):
    n_seq = lax.axis_size("seq")
    taps, kinds, channels = stem_weight.shape
    fits = lax.axis_size("section") == 2 and n_seq % 4 == 0 and depth_taps.shape[1] == 5
    fits = fits and bases.shape[1] == GROUP * 128 and (bases.shape[0] * GROUP) % 8 == 0
    fits = fits and channels % 256 == 0 and point_weight.shape[1] % BLOCK == 0
    fits = fits and kinds == 4 and taps * kinds <= 128
    run = fused if fits else shards
    return run(bases, stem_weight, gains, depth_taps, point_weight)


def solution(mesh):
    return jax.shard_map(
        chosen,
        mesh=mesh,
        in_specs=(
            P(None, "seq"),
            P(),
            P("section", None),
            P("section", None, None),
            P("section", "seq", None),
        ),
        out_specs=P(None, "seq", "section"),
        check_vma=False,
    )
```

```python
import functools

import jax
import jax.numpy as jnp
from jax import lax
from jax.experimental import pallas as pl
from jax.experimental.pallas import tpu as pltpu
from jax.sharding import PartitionSpec as P

DILATION_STEP = 2


def padded(array, sides, width):
    for axis, dim in sides:
        size, length = (lax.axis_size(axis), array.shape[dim])
        up = [(i, (i + 1) % size) for i in range(size - 1)]
        down = [(j, i) for i, j in up]
        last = lax.slice_in_dim(array, length - width, length, axis=dim)
        first = lax.slice_in_dim(array, 0, width, axis=dim)
        before = lax.ppermute(last, axis, up)
        after = lax.ppermute(first, axis, down)
        array = jnp.concatenate([before, array, after], axis=dim)
    return array


def shortened(array):

    def short(part):
        return part.astype(jnp.bfloat16) if part.dtype == jnp.float32 else part

    return jax.tree.map(short, array)


def passed_along(array, axis, by):
    length = lax.axis_size(axis)
    pairs = [(i, i + by) for i in range(length) if 0 <= i + by < length]
    return lax.ppermute(array, axis, pairs)


def from_root(value, axis, source):
    kept = jnp.where(lax.axis_index(axis) == source, value, 0).astype(value.dtype)
    return lax.psum(kept, axis)


def normalize_gelu(rows, gain_row):
    values = rows.astype(jnp.float32)
    square_mean = jnp.mean(values * values, axis=-1, keepdims=True)
    scaled = values * lax.rsqrt(square_mean + 1e-06) * gain_row.astype(jnp.float32)
    return jax.nn.gelu(scaled, approximate=True).astype(jnp.bfloat16)


def filter_rows(extended_rows, kernel_weight, length_total):
    summed = jnp.zeros((length_total, extended_rows.shape[1]), jnp.float32)
    for offset_amount in range(kernel_weight.shape[0]):
        window_rows = extended_rows[
            offset_amount * DILATION_STEP : offset_amount * DILATION_STEP + length_total
        ].astype(jnp.float32)
        summed = summed + kernel_weight[offset_amount].astype(jnp.float32) * window_rows
    return summed.astype(jnp.bfloat16)


def halve_rows(rows):
    return jnp.max(rows.reshape(rows.shape[0] // 2, 2, rows.shape[1]), axis=1)


def stem_rows(extended_ids, stem_weight, length_total):
    one_hot = (extended_ids[:, None] == jnp.arange(1, 5, dtype=jnp.int32)[None, :]).astype(
        jnp.bfloat16
    )
    window_rows = jnp.concatenate(
        [
            one_hot[offset_amount : offset_amount + length_total]
            for offset_amount in range(stem_weight.shape[0])
        ],
        axis=1,
    )
    flat = stem_weight.reshape(stem_weight.shape[0] * 4, stem_weight.shape[2])
    return jnp.dot(window_rows, flat, preferred_element_type=jnp.float32).astype(jnp.bfloat16)


def shards(bases, stem_weight, gains, depth_taps, point_weight):
    section_count = lax.axis_size("section")
    position = lax.axis_index("section")
    sequences, width_rows = bases.shape
    channels = stem_weight.shape[2]
    margin = stem_weight.shape[0] // 2
    padded_ids = padded(bases + 1, (("seq", 1),), margin)
    stems = jnp.stack(
        [stem_rows(padded_ids[index], stem_weight, width_rows) for index in range(sequences)]
    )
    gain_row = gains[0]
    kernel_weight = depth_taps[0]
    spread_width = kernel_weight.shape[0] // 2 * DILATION_STEP
    half_rows = width_rows // 2
    final_rows = width_rows >> section_count
    steps_total = sequences + section_count - 1
    first_section = position == 0
    valid_count = jnp.right_shift(jnp.int32(width_rows), position)

    def edge_rims(stem_now, inbox):
        head = jnp.where(first_section, stem_now[:spread_width], inbox[:spread_width])
        inbox_tail = lax.dynamic_slice_in_dim(inbox, valid_count - spread_width, spread_width, 0)
        tail = jnp.where(first_section, stem_now[width_rows - spread_width :], inbox_tail)
        edges = jnp.concatenate([head, tail], axis=0)
        framed = padded(normalize_gelu(edges, gain_row), (("seq", 0),), spread_width)
        return (framed[:spread_width], framed[3 * spread_width :])

    def prepare(level_rows, left_rim, right_rim):
        activated = normalize_gelu(level_rows, gain_row)
        extended_rows = jnp.concatenate([left_rim, activated, right_rim], axis=0)
        return filter_rows(extended_rows, kernel_weight, level_rows.shape[0])

    def complete(level_rows, product):
        pooled = halve_rows((level_rows.astype(jnp.float32) + product).astype(jnp.bfloat16))
        if pooled.shape[0] < half_rows:
            pooled = jnp.concatenate(
                [pooled, jnp.zeros((half_rows - pooled.shape[0], channels), jnp.bfloat16)], axis=0
            )
        return pooled

    def pass_on(pooled):
        return jax.tree.map(
            lambda part, own: part.astype(own.dtype),
            passed_along(shortened(pooled), "section", 1),
            pooled,
        )

    inbox_start = jnp.zeros((half_rows, channels), jnp.bfloat16)
    first_rows = stems[0]
    left_first, right_first = edge_rims(first_rows, inbox_start)
    filtered_first = prepare(first_rows, left_first, right_first)
    weights_full = lax.all_gather(point_weight, "seq", axis=1, tiled=True)[0]
    product_first = jnp.dot(filtered_first, weights_full, preferred_element_type=jnp.float32)
    inbox = pass_on(complete(first_rows, product_first))
    outbox = jnp.zeros((sequences, final_rows, channels), jnp.bfloat16)

    def make_level(level):
        count = width_rows >> level

        def run(operands):
            stem_now, inbox_now, left_rim, right_rim = operands
            level_rows = stem_now if level == 0 else inbox_now[:count]
            filtered = prepare(level_rows, left_rim, right_rim)
            product = jnp.dot(filtered, weights_full, preferred_element_type=jnp.float32)
            return complete(level_rows, product)

        return run

    branches = [make_level(level) for level in range(section_count)]

    def advance(inbox_now, outbox_now, step_index):
        micro_index = step_index - position
        live = (micro_index >= 0) & (micro_index < sequences)
        clipped = jnp.clip(micro_index, 0, sequences - 1)
        stem_now = lax.dynamic_index_in_dim(stems, clipped, 0, keepdims=False)
        left_rim, right_rim = edge_rims(stem_now, inbox_now)

        def working(operands):
            return lax.switch(position, branches, operands)

        def resting(operands):
            return jnp.zeros((half_rows, channels), jnp.bfloat16)

        pooled = lax.cond(live, working, resting, (stem_now, inbox_now, left_rim, right_rim))
        keep = live & (position == section_count - 1)
        updated = lax.dynamic_update_index_in_dim(outbox_now, pooled[:final_rows], clipped, 0)
        return (pooled, jnp.where(keep, updated, outbox_now))

    def middle_step(carry, step_index):
        pooled, outbox_next = advance(carry[0], carry[1], step_index)
        return ((pass_on(pooled), outbox_next), None)

    (inbox, outbox), unused = lax.scan(
        middle_step, (inbox, outbox), jnp.arange(1, steps_total - 1, dtype=jnp.int32)
    )
    pooled_last, outbox = advance(inbox, outbox, jnp.int32(steps_total - 1))
    coarsest = from_root(outbox, "section", section_count - 1)
    out_width = channels // section_count
    return lax.dynamic_slice_in_dim(coarsest, position * out_width, out_width, 2)


GROUP = 4
BLOCK = 16
PART = 48
MESH = pl.DeviceIdType.MESH


def gelu_of(scaled):
    inner = scaled * (0.7978845608028654 + 0.03567740813636141 * (scaled * scaled))
    return (0.5 * scaled) * (1.0 + jnp.tanh(inner))


def encoder_kernel(
    n_seq,
    bases_ref,
    stem_ref,
    gains_ref,
    taps_ref,
    weight_ref,
    out_ref,
    ids_all,
    params_all,
    stem_wide,
    stem_flat,
    one_hot,
    one_hot_rows,
    window,
    x0_buf,
    act_buf,
    d0_buf,
    x1_buf,
    d1_buf,
    weights,
    stage,
    send_sem,
    recv_sem,
    pair_send,
    pair_recv,
    side_send,
    side_recv,
    local_sem,
    out_send,
    out_recv,
):
    j = lax.axis_index("section")
    q = lax.axis_index("seq")
    n_z = n_seq // 4
    x, y, z = lax.rem(q, 2), lax.rem(lax.div(q, 2), 2), lax.div(q, 4)
    to_x, to_y = 1 - 2 * x, 2 * (1 - 2 * y)
    to_a = (1 - j) * to_x + j * to_y
    to_b = j * to_x + (1 - j) * to_y
    right, left = lax.rem(q + 1, n_seq), lax.rem(q + n_seq - 1, n_seq)
    other = 1 - j
    depth, width = weight_ref.shape[1], weight_ref.shape[2] // 2
    channels = 2 * width
    taps = stem_ref.shape[0]
    rows = x0_buf.shape[1]
    sequences, length = bases_ref.shape
    runs = length // GROUP
    margin = (rows - runs) // 2
    mine = sequences // 2
    def at_z(offset):
        return lax.rem(z + offset, n_z) * 4 + lax.rem(q, 4)

    barrier = pltpu.get_barrier_semaphore()
    greeted = [(other, q), (j, q + to_a), (j, q + to_b), (j, left), (j, right)]
    greeted += [(j, at_z(offset)) for offset in range(1, n_z)]
    for device in greeted:
        pl.semaphore_signal(barrier, inc=1, device_id=device, device_id_type=MESH)
    pl.semaphore_wait(barrier, len(greeted))

    def remote(src, dst, send, recv, device):
        return pltpu.make_async_remote_copy(
            src_ref=src,
            dst_ref=dst,
            send_sem=send,
            recv_sem=recv,
            device_id=device,
            device_id_type=MESH,
        )

    def chunk(level, index, half):
        start = pl.multiple_of(index * depth, BLOCK)
        return weights.at[level, half, pl.ds(start, depth)]

    def block(half):
        return weight_ref.at[0, :, half * width : (half + 1) * width]

    def other_block():
        return weight_ref.at[0, :, pl.ds(pl.multiple_of(other * width, 128), width)]

    def own_block():
        return weight_ref.at[0, :, pl.ds(pl.multiple_of(j * width, 128), width)]

    swap = [
        remote(src, chunk(j, q, h), side_send.at[n], side_recv.at[n], (other, q))
        for n, (src, h) in enumerate([(other_block(), other), (own_block(), j)])
    ]
    swapped = [
        remote(src, chunk(other, q, h), side_send.at[n], side_recv.at[n], (other, q))
        for n, (src, h) in enumerate([(own_block(), j), (other_block(), other)])
    ]
    local = [
        pltpu.make_async_copy(block(h), chunk(j, q, h), local_sem.at[h]) for h in range(2)
    ]
    edge = 128
    to_right = remote(
        bases_ref.at[:, length - edge :],
        ids_all.at[:, :edge],
        side_send.at[2],
        side_recv.at[2],
        (j, right),
    )
    to_left = remote(
        bases_ref.at[:, :edge],
        ids_all.at[:, edge + length :],
        side_send.at[3],
        side_recv.at[3],
        (j, left),
    )
    swap[0].start()
    to_right.start()
    to_left.start()
    for h in range(2):
        local[h].start()
    keep_ids = pltpu.make_async_copy(
        bases_ref, ids_all.at[:, edge : edge + length], local_sem.at[2]
    )
    keep_ids.start()
    params_all[j, 0:1, :] = gains_ref[...].astype(jnp.float32)
    params_all[j, 1:6, :] = taps_ref[0].astype(jnp.float32)
    share = remote(
        params_all.at[j], params_all.at[j], side_send.at[4], side_recv.at[4], (other, q)
    )
    shared = remote(
        params_all.at[other], params_all.at[other], side_send.at[4], side_recv.at[4], (other, q)
    )
    share.start()
    for h in range(2):
        local[h].wait()
    swapped[0].wait_recv()

    def z_copy(level, offset, incoming):
        index = at_z(n_z - offset) if incoming else q
        slot = offset - 1
        part = chunk(level, index, j)
        return remote(
            part, part, send_sem.at[level, slot], recv_sem.at[level, slot], (j, at_z(offset))
        )

    def a_copy(level, offset, incoming):
        index = at_z(n_z - offset) if offset else q
        slot = n_z - 1 + offset
        part = chunk(level, index + to_a if incoming else index, j)
        return remote(
            part, part, send_sem.at[level, slot], recv_sem.at[level, slot], (j, q + to_a)
        )

    def b_copy(level, offset, crossed, incoming):
        index = at_z(n_z - offset) if offset else q
        index = index + to_a if crossed else index
        slot = 2 * n_z - 1 + offset + (n_z if crossed else 0)
        part = chunk(level, index + to_b if incoming else index, j)
        return remote(
            part, part, send_sem.at[level, slot], recv_sem.at[level, slot], (j, q + to_b)
        )

    def pair_copy(level, index, slot, incoming):
        part = chunk(level, index, other if incoming else j)
        return remote(
            part, part, pair_send.at[level, slot], pair_recv.at[level, slot], (other, q)
        )

    def pair_index(slot, incoming):
        step_a, step_b = (to_b, to_a) if incoming else (to_a, to_b)
        if slot < n_z - 1:
            return at_z(n_z - slot - 1)
        offset = (slot - n_z + 1) % n_z
        index = at_z(n_z - offset) if offset else q
        kind = (slot - n_z + 1) // n_z
        return index + (step_a, step_b, step_a + step_b)[kind]

    def pair(level, slot, incoming=False):
        return pair_copy(level, pair_index(slot, incoming), slot, incoming)

    def pairs_in(level):
        for slot in range(4 * n_z - 1):
            pair(level, slot, True).wait_recv()

    def own(level):
        for offset in range(1, n_z):
            z_copy(level, offset, False).start()
        a_copy(level, 0, False).start()
        b_copy(level, 0, False, False).start()

    def z_event(level, offset):
        z_copy(level, offset, True).wait_recv()
        a_copy(level, offset, False).start()
        b_copy(level, offset, False, False).start()
        pair(level, offset - 1).start()

    def a_event(level, offset):
        a_copy(level, offset, True).wait_recv()
        b_copy(level, offset, True, False).start()
        pair(level, n_z - 1 + offset).start()

    def b_event(level, offset, crossed):
        b_copy(level, offset, crossed, True).wait_recv()
        pair(level, (3 * n_z - 1 if crossed else 2 * n_z - 1) + offset).start()

    def sends_done(level):
        for offset in range(1, n_z):
            z_copy(level, offset, False).wait_send()
        for offset in range(n_z):
            a_copy(level, offset, False).wait_send()
            b_copy(level, offset, False, False).wait_send()
            b_copy(level, offset, True, False).wait_send()
        for slot in range(4 * n_z - 1):
            pair(level, slot).wait_send()

    own(0)
    own(1)
    swap[1].start()

    stem_wide[...] = jnp.zeros_like(stem_wide)
    one_hot[...] = jnp.zeros_like(one_hot)
    for k in range(taps):
        stem_wide[4 * k : 4 * k + 4, :] = stem_ref[k].astype(jnp.float32)
    stem_flat[...] = stem_wide[...].astype(jnp.bfloat16)
    to_right.wait_recv()
    to_left.wait_recv()
    keep_ids.wait()
    lanes = ids_all.shape[1]
    span = one_hot.shape[1]
    four = lax.broadcasted_iota(jnp.int32, (4, span), 0)
    place = lax.broadcasted_iota(jnp.int32, (1, lanes), 1)
    inside = ((place >= edge) | (q > 0)) & ((place < edge + length) | (q < n_seq - 1))
    for b in range(mine):
        line = jnp.where(j == 0, ids_all[b : b + 1, :], ids_all[mine + b : mine + b + 1, :])
        line = jnp.where(inside, line, -1)
        for k in range(taps):
            begin = edge - GROUP * margin + k - taps // 2
            moved = pltpu.roll(line, lanes - begin, 1)[:, :span]
            hit = jnp.broadcast_to(moved, (4, span)) == four
            one_hot[4 * k : 4 * k + 4, :] = hit.astype(jnp.float32)
        one_hot_rows[...] = one_hot[...].T
        for c in range(GROUP):
            window[b * GROUP + c] = one_hot_rows[pl.ds(c, rows, stride=GROUP), :].astype(
                jnp.bfloat16
            )
    shared.wait_recv()

    def row_mask(start, total_low, total_high, count):
        index = lax.broadcasted_iota(jnp.int32, (count, 1), 0) + start
        return (index >= total_low) & (index < total_high)

    low = margin - q * runs
    high = low + n_seq * runs
    blocks = rows // PART
    inverse = 1.0 / channels

    def first_block(step, carry):
        stream = lax.div(step, blocks)
        start = pl.multiple_of(lax.rem(step, blocks) * PART, PART)
        part = pl.ds(start, PART)
        found = jnp.dot(
            window[stream, part, :], stem_flat[...], preferred_element_type=jnp.float32
        ).astype(jnp.bfloat16)
        x0_buf[stream, part, :] = found
        values = found.astype(jnp.float32)
        mean = jnp.sum(values * values, axis=1, keepdims=True) * inverse
        scaled = values * lax.rsqrt(mean + 1e-06) * params_all[0, 0:1, :]
        act_buf[stream, part, :] = jnp.where(
            row_mask(start, low, high, PART), gelu_of(scaled), 0.0
        )
        return carry

    col_blocks = channels // 128

    def first_filter(step, carry):
        col = pl.ds(pl.multiple_of(lax.rem(step, col_blocks) * 128, 128), 128)
        pair = lax.div(step, col_blocks)
        even = lax.div(pair, 2) * GROUP + lax.rem(pair, 2)
        odd = even + 2
        tap = [params_all[0, 1 + k : 2 + k, col] for k in range(5)]
        a0, a2 = act_buf[even, :, col], act_buf[odd, :, col]
        a0_before, a2_before = pltpu.roll(a0, 1, 0), pltpu.roll(a2, 1, 0)
        a0_after, a2_after = pltpu.roll(a0, rows - 1, 0), pltpu.roll(a2, rows - 1, 0)
        d0_buf[even, :, col] = (
            tap[0] * a0_before + tap[1] * a2_before + tap[2] * a0 + tap[3] * a2 + tap[4] * a0_after
        ).astype(jnp.bfloat16)
        d0_buf[odd, :, col] = (
            tap[0] * a2_before + tap[1] * a0 + tap[2] * a2 + tap[3] * a0_after + tap[4] * a2_after
        ).astype(jnp.bfloat16)
        return carry

    def interleaved(total, body, events):
        done = 0
        for number, event in enumerate(events):
            until = total * (number + 1) // (len(events) + 1)
            lax.fori_loop(done, until, body, 0)
            event()
            done = until
        lax.fori_loop(done, total, body, 0)

    def later(function, *args):
        return lambda: function(*args)

    z_events = [[later(z_event, level, o) for o in range(1, n_z)] for level in range(2)]
    a_events = [[later(a_event, level, o) for o in range(n_z)] for level in range(2)]

    b_early = [[later(b_event, level, o, False) for o in range(n_z)] for level in range(2)]
    b_late = [[later(b_event, level, o, True) for o in range(n_z)] for level in range(2)]
    interleaved(mine * GROUP * blocks, first_block, z_events[0] + a_events[0])
    interleaved(
        mine * 2 * col_blocks, first_filter, z_events[1] + b_early[0] + a_events[1] + b_late[0]
    )

    swapped[1].wait_recv()
    pairs_in(0)
    rest = b_early[1] + b_late[1]
    for stream in range(2 * mine):
        for h in range(2):
            taken = d0_buf[2 * stream : 2 * stream + 2].reshape(2 * rows, channels)
            product = jnp.dot(taken, weights[0, h], preferred_element_type=jnp.float32)
            level_rows = x0_buf[2 * stream : 2 * stream + 2, :, h * width : (h + 1) * width]
            level_rows = level_rows.reshape(2 * rows, width)
            mixed = (level_rows.astype(jnp.float32) + product).astype(jnp.bfloat16)
            x1_buf[stream, :, h * width : (h + 1) * width] = jnp.maximum(
                mixed[:rows], mixed[rows:]
            )
            if rest:
                rest.pop(0)()

    def second_block(stream):
        def run(step, carry):
            start = pl.multiple_of(step * PART, PART)
            part = pl.ds(start, PART)
            values = x1_buf[stream, part, :].astype(jnp.float32)
            mean = jnp.sum(values * values, axis=1, keepdims=True) * inverse
            scaled = values * lax.rsqrt(mean + 1e-06) * params_all[1, 0:1, :]
            act_buf[stream, part, :] = jnp.where(
                row_mask(start, low, high, PART), gelu_of(scaled), 0.0
            )
            return carry

        return run

    def second_filter(stream):
        def run(step, carry):
            col = pl.ds(pl.multiple_of(step * 128, 128), 128)
            tap = [params_all[1, 1 + k : 2 + k, col] for k in range(5)]
            a = act_buf[stream, :, col]
            total = tap[2] * a
            for k in (0, 1, 3, 4):
                total = total + tap[k] * pltpu.roll(a, (2 - k) % rows, 0)
            d1_buf[stream, :, col] = total[margin : margin + runs].astype(jnp.bfloat16)
            return carry

        return run

    for stream in range(2 * mine):
        lax.fori_loop(0, blocks, second_block(stream), 0)
        if rest:
            rest.pop(0)()
        lax.fori_loop(0, col_blocks, second_filter(stream), 0)
    for event in rest:
        event()

    def out_copy(b, incoming):
        return remote(
            stage.at[other, b],
            out_ref.at[(other if incoming else j) * mine + b],
            out_send.at[b],
            out_recv.at[b],
            (other, q),
        )

    pairs_in(1)
    for b in range(mine):
        for h in range(2):
            taken = d1_buf[2 * b : 2 * b + 2].reshape(2 * runs, channels)
            product = jnp.dot(taken, weights[1, h], preferred_element_type=jnp.float32)
            level_rows = x1_buf[
                2 * b : 2 * b + 2, margin : margin + runs, h * width : (h + 1) * width
            ].reshape(2 * runs, width)
            mixed = (level_rows.astype(jnp.float32) + product).astype(jnp.bfloat16)
            stage[h, b] = jnp.maximum(mixed[:runs], mixed[runs:])
        out_copy(b, False).start()
        out_ref[j * mine + b] = stage[j, b]

    for b in range(mine):
        out_copy(b, True).wait_recv()
        out_copy(b, False).wait_send()
    for copy in swap:
        copy.wait_send()
    to_right.wait_send()
    to_left.wait_send()
    share.wait_send()
    sends_done(0)
    sends_done(1)


def fused(bases, stem_weight, gains, depth_taps, point_weight):
    n_seq = lax.axis_size("seq")
    sequences, width_rows = bases.shape
    channels = stem_weight.shape[2]
    runs = width_rows // GROUP
    rows = runs + BLOCK
    streams = sequences // 2 * GROUP
    half = channels // 2
    n_z = n_seq // 4
    slots = 4 * n_z - 1
    vmem = pl.BlockSpec(memory_space=pltpu.VMEM)
    dma = pltpu.SemaphoreType.DMA
    return pl.pallas_call(
        functools.partial(encoder_kernel, n_seq),
        out_shape=jax.ShapeDtypeStruct((sequences, runs, half), jnp.bfloat16),
        in_specs=[vmem] * 5,
        out_specs=vmem,
        scratch_shapes=[
            pltpu.VMEM((sequences, width_rows + 256), jnp.int32),
            pltpu.VMEM((2, 8, channels), jnp.float32),
            pltpu.VMEM((128, channels), jnp.float32),
            pltpu.VMEM((128, channels), jnp.bfloat16),
            pltpu.VMEM((128, width_rows + 128), jnp.float32),
            pltpu.VMEM((width_rows + 128, 128), jnp.float32),
            pltpu.VMEM((streams, rows, 128), jnp.bfloat16),
            pltpu.VMEM((streams, rows, channels), jnp.bfloat16),
            pltpu.VMEM((streams, rows, channels), jnp.float32),
            pltpu.VMEM((streams, rows, channels), jnp.bfloat16),
            pltpu.VMEM((streams // 2, rows, channels), jnp.bfloat16),
            pltpu.VMEM((streams // 2, runs, channels), jnp.bfloat16),
            pltpu.VMEM((2, 2, channels, half), jnp.bfloat16),
            pltpu.VMEM((2, sequences // 2, runs, half), jnp.bfloat16),
            dma((2, slots)),
            dma((2, slots)),
            dma((2, slots)),
            dma((2, slots)),
            dma((5,)),
            dma((5,)),
            dma((3,)),
            dma((sequences // 2,)),
            dma((sequences // 2,)),
        ],
        compiler_params=pltpu.CompilerParams(
            collective_id=0, has_side_effects=True, vmem_limit_bytes=56 * 1024 * 1024
        ),
    )(bases, stem_weight, gains, depth_taps, point_weight)


def chosen(bases, stem_weight, gains, depth_taps, point_weight):
    n_seq = lax.axis_size("seq")
    taps, kinds, channels = stem_weight.shape
    fits = lax.axis_size("section") == 2 and n_seq % 4 == 0 and depth_taps.shape[1] == 5
    fits = fits and bases.shape[1] == GROUP * 128 and bases.shape[0] % 2 == 0
    fits = fits and channels % 256 == 0 and point_weight.shape[1] % BLOCK == 0
    fits = fits and kinds == 4 and taps * kinds <= 128
    run = fused if fits else shards
    return run(bases, stem_weight, gains, depth_taps, point_weight)


def solution(mesh):
    return jax.shard_map(
        chosen,
        mesh=mesh,
        in_specs=(
            P(None, "seq"),
            P(),
            P("section", None),
            P("section", None, None),
            P("section", "seq", None),
        ),
        out_specs=P(None, "seq", "section"),
        check_vma=False,
    )
```

```python
import functools

import jax
import jax.numpy as jnp
from jax import lax
from jax.experimental import pallas as pl
from jax.experimental.pallas import tpu as pltpu
from jax.sharding import PartitionSpec as P

DILATION_STEP = 2


def padded(array, sides, width):
    for axis, dim in sides:
        size, length = (lax.axis_size(axis), array.shape[dim])
        up = [(i, (i + 1) % size) for i in range(size - 1)]
        down = [(j, i) for i, j in up]
        last = lax.slice_in_dim(array, length - width, length, axis=dim)
        first = lax.slice_in_dim(array, 0, width, axis=dim)
        before = lax.ppermute(last, axis, up)
        after = lax.ppermute(first, axis, down)
        array = jnp.concatenate([before, array, after], axis=dim)
    return array


def shortened(array):

    def short(part):
        return part.astype(jnp.bfloat16) if part.dtype == jnp.float32 else part

    return jax.tree.map(short, array)


def passed_along(array, axis, by):
    length = lax.axis_size(axis)
    pairs = [(i, i + by) for i in range(length) if 0 <= i + by < length]
    return lax.ppermute(array, axis, pairs)


def from_root(value, axis, source):
    kept = jnp.where(lax.axis_index(axis) == source, value, 0).astype(value.dtype)
    return lax.psum(kept, axis)


def normalize_gelu(rows, gain_row):
    values = rows.astype(jnp.float32)
    square_mean = jnp.mean(values * values, axis=-1, keepdims=True)
    scaled = values * lax.rsqrt(square_mean + 1e-06) * gain_row.astype(jnp.float32)
    return jax.nn.gelu(scaled, approximate=True).astype(jnp.bfloat16)


def filter_rows(extended_rows, kernel_weight, length_total):
    summed = jnp.zeros((length_total, extended_rows.shape[1]), jnp.float32)
    for offset_amount in range(kernel_weight.shape[0]):
        window_rows = extended_rows[
            offset_amount * DILATION_STEP : offset_amount * DILATION_STEP + length_total
        ].astype(jnp.float32)
        summed = summed + kernel_weight[offset_amount].astype(jnp.float32) * window_rows
    return summed.astype(jnp.bfloat16)


def halve_rows(rows):
    return jnp.max(rows.reshape(rows.shape[0] // 2, 2, rows.shape[1]), axis=1)


def stem_rows(extended_ids, stem_weight, length_total):
    one_hot = (extended_ids[:, None] == jnp.arange(1, 5, dtype=jnp.int32)[None, :]).astype(
        jnp.bfloat16
    )
    window_rows = jnp.concatenate(
        [
            one_hot[offset_amount : offset_amount + length_total]
            for offset_amount in range(stem_weight.shape[0])
        ],
        axis=1,
    )
    flat = stem_weight.reshape(stem_weight.shape[0] * 4, stem_weight.shape[2])
    return jnp.dot(window_rows, flat, preferred_element_type=jnp.float32).astype(jnp.bfloat16)


def shards(bases, stem_weight, gains, depth_taps, point_weight):
    section_count = lax.axis_size("section")
    position = lax.axis_index("section")
    sequences, width_rows = bases.shape
    channels = stem_weight.shape[2]
    margin = stem_weight.shape[0] // 2
    padded_ids = padded(bases + 1, (("seq", 1),), margin)
    stems = jnp.stack(
        [stem_rows(padded_ids[index], stem_weight, width_rows) for index in range(sequences)]
    )
    gain_row = gains[0]
    kernel_weight = depth_taps[0]
    spread_width = kernel_weight.shape[0] // 2 * DILATION_STEP
    half_rows = width_rows // 2
    final_rows = width_rows >> section_count
    steps_total = sequences + section_count - 1
    first_section = position == 0
    valid_count = jnp.right_shift(jnp.int32(width_rows), position)

    def edge_rims(stem_now, inbox):
        head = jnp.where(first_section, stem_now[:spread_width], inbox[:spread_width])
        inbox_tail = lax.dynamic_slice_in_dim(inbox, valid_count - spread_width, spread_width, 0)
        tail = jnp.where(first_section, stem_now[width_rows - spread_width :], inbox_tail)
        edges = jnp.concatenate([head, tail], axis=0)
        framed = padded(normalize_gelu(edges, gain_row), (("seq", 0),), spread_width)
        return (framed[:spread_width], framed[3 * spread_width :])

    def prepare(level_rows, left_rim, right_rim):
        activated = normalize_gelu(level_rows, gain_row)
        extended_rows = jnp.concatenate([left_rim, activated, right_rim], axis=0)
        return filter_rows(extended_rows, kernel_weight, level_rows.shape[0])

    def complete(level_rows, product):
        pooled = halve_rows((level_rows.astype(jnp.float32) + product).astype(jnp.bfloat16))
        if pooled.shape[0] < half_rows:
            pooled = jnp.concatenate(
                [pooled, jnp.zeros((half_rows - pooled.shape[0], channels), jnp.bfloat16)], axis=0
            )
        return pooled

    def pass_on(pooled):
        return jax.tree.map(
            lambda part, own: part.astype(own.dtype),
            passed_along(shortened(pooled), "section", 1),
            pooled,
        )

    inbox_start = jnp.zeros((half_rows, channels), jnp.bfloat16)
    first_rows = stems[0]
    left_first, right_first = edge_rims(first_rows, inbox_start)
    filtered_first = prepare(first_rows, left_first, right_first)
    weights_full = lax.all_gather(point_weight, "seq", axis=1, tiled=True)[0]
    product_first = jnp.dot(filtered_first, weights_full, preferred_element_type=jnp.float32)
    inbox = pass_on(complete(first_rows, product_first))
    outbox = jnp.zeros((sequences, final_rows, channels), jnp.bfloat16)

    def make_level(level):
        count = width_rows >> level

        def run(operands):
            stem_now, inbox_now, left_rim, right_rim = operands
            level_rows = stem_now if level == 0 else inbox_now[:count]
            filtered = prepare(level_rows, left_rim, right_rim)
            product = jnp.dot(filtered, weights_full, preferred_element_type=jnp.float32)
            return complete(level_rows, product)

        return run

    branches = [make_level(level) for level in range(section_count)]

    def advance(inbox_now, outbox_now, step_index):
        micro_index = step_index - position
        live = (micro_index >= 0) & (micro_index < sequences)
        clipped = jnp.clip(micro_index, 0, sequences - 1)
        stem_now = lax.dynamic_index_in_dim(stems, clipped, 0, keepdims=False)
        left_rim, right_rim = edge_rims(stem_now, inbox_now)

        def working(operands):
            return lax.switch(position, branches, operands)

        def resting(operands):
            return jnp.zeros((half_rows, channels), jnp.bfloat16)

        pooled = lax.cond(live, working, resting, (stem_now, inbox_now, left_rim, right_rim))
        keep = live & (position == section_count - 1)
        updated = lax.dynamic_update_index_in_dim(outbox_now, pooled[:final_rows], clipped, 0)
        return (pooled, jnp.where(keep, updated, outbox_now))

    def middle_step(carry, step_index):
        pooled, outbox_next = advance(carry[0], carry[1], step_index)
        return ((pass_on(pooled), outbox_next), None)

    (inbox, outbox), unused = lax.scan(
        middle_step, (inbox, outbox), jnp.arange(1, steps_total - 1, dtype=jnp.int32)
    )
    pooled_last, outbox = advance(inbox, outbox, jnp.int32(steps_total - 1))
    coarsest = from_root(outbox, "section", section_count - 1)
    out_width = channels // section_count
    return lax.dynamic_slice_in_dim(coarsest, position * out_width, out_width, 2)


GROUP = 4
BLOCK = 16
PART = 48
MESH = pl.DeviceIdType.MESH


def gelu_of(scaled):
    inner = scaled * (0.7978845608028654 + 0.03567740813636141 * (scaled * scaled))
    return (0.5 * scaled) * (1.0 + jnp.tanh(inner))


def encoder_kernel(
    n_seq,
    bases_ref,
    stem_ref,
    gains_ref,
    taps_ref,
    weight_ref,
    out_ref,
    ids_all,
    params_all,
    stem_wide,
    stem_flat,
    one_hot,
    one_hot_rows,
    window,
    x0_buf,
    act_buf,
    d0_buf,
    x1_buf,
    d1_buf,
    weights,
    stage,
    send_sem,
    recv_sem,
    pair_send,
    pair_recv,
    side_send,
    side_recv,
    local_sem,
    out_send,
    out_recv,
):
    j = lax.axis_index("section")
    q = lax.axis_index("seq")
    n_z = n_seq // 4
    x, y, z = lax.rem(q, 2), lax.rem(lax.div(q, 2), 2), lax.div(q, 4)
    to_x, to_y = 1 - 2 * x, 2 * (1 - 2 * y)
    to_a = (1 - j) * to_x + j * to_y
    to_b = j * to_x + (1 - j) * to_y
    right, left = lax.rem(q + 1, n_seq), lax.rem(q + n_seq - 1, n_seq)
    other = 1 - j
    depth, width = weight_ref.shape[1], weight_ref.shape[2] // 2
    channels = 2 * width
    taps = stem_ref.shape[0]
    rows = x0_buf.shape[1]
    sequences, length = bases_ref.shape
    runs = length // GROUP
    margin = (rows - runs) // 2
    mine = sequences // 2
    def at_z(offset):
        return lax.rem(z + offset, n_z) * 4 + lax.rem(q, 4)

    barrier = pltpu.get_barrier_semaphore()
    greeted = [(other, q), (j, q + to_a), (j, q + to_b), (j, left), (j, right)]
    greeted += [(j, at_z(offset)) for offset in range(1, n_z)]
    for device in greeted:
        pl.semaphore_signal(barrier, inc=1, device_id=device, device_id_type=MESH)
    pl.semaphore_wait(barrier, len(greeted))

    def remote(src, dst, send, recv, device):
        return pltpu.make_async_remote_copy(
            src_ref=src,
            dst_ref=dst,
            send_sem=send,
            recv_sem=recv,
            device_id=device,
            device_id_type=MESH,
        )

    def chunk(level, index, half):
        start = pl.multiple_of(index * depth, BLOCK)
        return weights.at[level, half, pl.ds(start, depth)]

    def block(half):
        return weight_ref.at[0, :, half * width : (half + 1) * width]

    def other_block():
        return weight_ref.at[0, :, pl.ds(pl.multiple_of(other * width, 128), width)]

    def own_block():
        return weight_ref.at[0, :, pl.ds(pl.multiple_of(j * width, 128), width)]

    swap = [
        remote(src, chunk(j, q, h), side_send.at[n], side_recv.at[n], (other, q))
        for n, (src, h) in enumerate([(other_block(), other), (own_block(), j)])
    ]
    swapped = [
        remote(src, chunk(other, q, h), side_send.at[n], side_recv.at[n], (other, q))
        for n, (src, h) in enumerate([(own_block(), j), (other_block(), other)])
    ]
    local = [
        pltpu.make_async_copy(block(h), chunk(j, q, h), local_sem.at[h]) for h in range(2)
    ]
    edge = 128
    to_right = remote(
        bases_ref.at[:, length - edge :],
        ids_all.at[:, :edge],
        side_send.at[2],
        side_recv.at[2],
        (j, right),
    )
    to_left = remote(
        bases_ref.at[:, :edge],
        ids_all.at[:, edge + length :],
        side_send.at[3],
        side_recv.at[3],
        (j, left),
    )
    swap[0].start()
    to_right.start()
    to_left.start()
    for h in range(2):
        local[h].start()
    keep_ids = pltpu.make_async_copy(
        bases_ref, ids_all.at[:, edge : edge + length], local_sem.at[2]
    )
    keep_ids.start()
    params_all[j, 0:1, :] = gains_ref[...].astype(jnp.float32)
    params_all[j, 1:6, :] = taps_ref[0].astype(jnp.float32)
    share = remote(
        params_all.at[j], params_all.at[j], side_send.at[4], side_recv.at[4], (other, q)
    )
    shared = remote(
        params_all.at[other], params_all.at[other], side_send.at[4], side_recv.at[4], (other, q)
    )
    share.start()
    for h in range(2):
        local[h].wait()
    swapped[0].wait_recv()

    def z_copy(level, offset, incoming):
        index = at_z(n_z - offset) if incoming else q
        slot = offset - 1
        part = chunk(level, index, j)
        return remote(
            part, part, send_sem.at[level, slot], recv_sem.at[level, slot], (j, at_z(offset))
        )

    def a_copy(level, offset, incoming):
        index = at_z(n_z - offset) if offset else q
        slot = n_z - 1 + offset
        part = chunk(level, index + to_a if incoming else index, j)
        return remote(
            part, part, send_sem.at[level, slot], recv_sem.at[level, slot], (j, q + to_a)
        )

    def b_copy(level, offset, crossed, incoming):
        index = at_z(n_z - offset) if offset else q
        index = index + to_a if crossed else index
        slot = 2 * n_z - 1 + offset + (n_z if crossed else 0)
        part = chunk(level, index + to_b if incoming else index, j)
        return remote(
            part, part, send_sem.at[level, slot], recv_sem.at[level, slot], (j, q + to_b)
        )

    def pair_copy(level, index, slot, incoming):
        part = chunk(level, index, other if incoming else j)
        return remote(
            part, part, pair_send.at[level, slot], pair_recv.at[level, slot], (other, q)
        )

    def pair_index(slot, incoming):
        step_a, step_b = (to_b, to_a) if incoming else (to_a, to_b)
        if slot < n_z - 1:
            return at_z(n_z - slot - 1)
        offset = (slot - n_z + 1) % n_z
        index = at_z(n_z - offset) if offset else q
        kind = (slot - n_z + 1) // n_z
        return index + (step_a, step_b, step_a + step_b)[kind]

    def pair(level, slot, incoming=False):
        return pair_copy(level, pair_index(slot, incoming), slot, incoming)

    def pairs_in(level):
        for slot in range(4 * n_z - 1):
            pair(level, slot, True).wait_recv()

    def own(level):
        for offset in range(1, n_z):
            z_copy(level, offset, False).start()
        a_copy(level, 0, False).start()
        b_copy(level, 0, False, False).start()

    def z_event(level, offset):
        z_copy(level, offset, True).wait_recv()
        a_copy(level, offset, False).start()
        b_copy(level, offset, False, False).start()
        pair(level, offset - 1).start()

    def a_event(level, offset):
        a_copy(level, offset, True).wait_recv()
        b_copy(level, offset, True, False).start()
        pair(level, n_z - 1 + offset).start()

    def b_event(level, offset, crossed):
        b_copy(level, offset, crossed, True).wait_recv()
        pair(level, (3 * n_z - 1 if crossed else 2 * n_z - 1) + offset).start()

    def sends_done(level):
        for offset in range(1, n_z):
            z_copy(level, offset, False).wait_send()
        for offset in range(n_z):
            a_copy(level, offset, False).wait_send()
            b_copy(level, offset, False, False).wait_send()
            b_copy(level, offset, True, False).wait_send()
        for slot in range(4 * n_z - 1):
            pair(level, slot).wait_send()

    own(0)
    swap[1].start()

    stem_wide[...] = jnp.zeros_like(stem_wide)
    one_hot[...] = jnp.zeros_like(one_hot)
    for k in range(taps):
        stem_wide[4 * k : 4 * k + 4, :] = stem_ref[k].astype(jnp.float32)
    stem_flat[...] = stem_wide[...].astype(jnp.bfloat16)
    to_right.wait_recv()
    to_left.wait_recv()
    keep_ids.wait()
    lanes = ids_all.shape[1]
    span = one_hot.shape[1]
    four = lax.broadcasted_iota(jnp.int32, (4, span), 0)
    place = lax.broadcasted_iota(jnp.int32, (1, lanes), 1)
    inside = ((place >= edge) | (q > 0)) & ((place < edge + length) | (q < n_seq - 1))
    for b in range(mine):
        line = jnp.where(j == 0, ids_all[b : b + 1, :], ids_all[mine + b : mine + b + 1, :])
        line = jnp.where(inside, line, -1)
        for k in range(taps):
            begin = edge - GROUP * margin + k - taps // 2
            moved = pltpu.roll(line, lanes - begin, 1)[:, :span]
            hit = jnp.broadcast_to(moved, (4, span)) == four
            one_hot[4 * k : 4 * k + 4, :] = hit.astype(jnp.float32)
        one_hot_rows[...] = one_hot[...].T
        for c in range(GROUP):
            window[b * GROUP + c] = one_hot_rows[pl.ds(c, rows, stride=GROUP), :].astype(
                jnp.bfloat16
            )
    shared.wait_recv()

    def row_mask(start, total_low, total_high, count):
        index = lax.broadcasted_iota(jnp.int32, (count, 1), 0) + start
        return (index >= total_low) & (index < total_high)

    low = margin - q * runs
    high = low + n_seq * runs
    blocks = rows // PART
    inverse = 1.0 / channels

    def first_block(step, carry):
        stream = lax.div(step, blocks)
        start = pl.multiple_of(lax.rem(step, blocks) * PART, PART)
        part = pl.ds(start, PART)
        found = jnp.dot(
            window[stream, part, :], stem_flat[...], preferred_element_type=jnp.float32
        ).astype(jnp.bfloat16)
        x0_buf[stream, part, :] = found
        values = found.astype(jnp.float32)
        mean = jnp.sum(values * values, axis=1, keepdims=True) * inverse
        scaled = values * lax.rsqrt(mean + 1e-06) * params_all[0, 0:1, :]
        act_buf[stream, part, :] = jnp.where(
            row_mask(start, low, high, PART), gelu_of(scaled), 0.0
        )
        return carry

    col_blocks = channels // 128

    def first_filter(step, carry):
        col = pl.ds(pl.multiple_of(lax.rem(step, col_blocks) * 128, 128), 128)
        pair = lax.div(step, col_blocks)
        even = lax.div(pair, 2) * GROUP + lax.rem(pair, 2)
        odd = even + 2
        tap = [params_all[0, 1 + k : 2 + k, col] for k in range(5)]
        a0, a2 = act_buf[even, :, col], act_buf[odd, :, col]
        a0_before, a2_before = pltpu.roll(a0, 1, 0), pltpu.roll(a2, 1, 0)
        a0_after, a2_after = pltpu.roll(a0, rows - 1, 0), pltpu.roll(a2, rows - 1, 0)
        d0_buf[even, :, col] = (
            tap[0] * a0_before + tap[1] * a2_before + tap[2] * a0 + tap[3] * a2 + tap[4] * a0_after
        ).astype(jnp.bfloat16)
        d0_buf[odd, :, col] = (
            tap[0] * a2_before + tap[1] * a0 + tap[2] * a2 + tap[3] * a0_after + tap[4] * a2_after
        ).astype(jnp.bfloat16)
        return carry

    def interleaved(total, body, events):
        done = 0
        for number, event in enumerate(events):
            until = total * (number + 1) // (len(events) + 1)
            lax.fori_loop(done, until, body, 0)
            event()
            done = until
        lax.fori_loop(done, total, body, 0)

    def later(function, *args):
        return lambda: function(*args)

    z_events = [[later(z_event, level, o) for o in range(1, n_z)] for level in range(2)]
    a_events = [[later(a_event, level, o) for o in range(n_z)] for level in range(2)]

    b_early = [[later(b_event, level, o, False) for o in range(n_z)] for level in range(2)]
    b_late = [[later(b_event, level, o, True) for o in range(n_z)] for level in range(2)]
    interleaved(mine * GROUP * blocks, first_block, z_events[0] + [later(own, 1)] + a_events[0])
    interleaved(
        mine * 2 * col_blocks, first_filter, z_events[1] + b_early[0] + a_events[1] + b_late[0]
    )

    swapped[1].wait_recv()
    pairs_in(0)
    rest = b_early[1] + b_late[1]
    for stream in range(2 * mine):
        for h in range(2):
            taken = d0_buf[2 * stream : 2 * stream + 2].reshape(2 * rows, channels)
            product = jnp.dot(taken, weights[0, h], preferred_element_type=jnp.float32)
            level_rows = x0_buf[2 * stream : 2 * stream + 2, :, h * width : (h + 1) * width]
            level_rows = level_rows.reshape(2 * rows, width)
            mixed = (level_rows.astype(jnp.float32) + product).astype(jnp.bfloat16)
            x1_buf[stream, :, h * width : (h + 1) * width] = jnp.maximum(
                mixed[:rows], mixed[rows:]
            )
            if rest:
                rest.pop(0)()

    def second_block(stream):
        def run(step, carry):
            start = pl.multiple_of(step * PART, PART)
            part = pl.ds(start, PART)
            values = x1_buf[stream, part, :].astype(jnp.float32)
            mean = jnp.sum(values * values, axis=1, keepdims=True) * inverse
            scaled = values * lax.rsqrt(mean + 1e-06) * params_all[1, 0:1, :]
            act_buf[stream, part, :] = jnp.where(
                row_mask(start, low, high, PART), gelu_of(scaled), 0.0
            )
            return carry

        return run

    def second_filter(stream):
        def run(step, carry):
            col = pl.ds(pl.multiple_of(step * 128, 128), 128)
            tap = [params_all[1, 1 + k : 2 + k, col] for k in range(5)]
            a = act_buf[stream, :, col]
            total = tap[2] * a
            for k in (0, 1, 3, 4):
                total = total + tap[k] * pltpu.roll(a, (2 - k) % rows, 0)
            d1_buf[stream, :, col] = total[margin : margin + runs].astype(jnp.bfloat16)
            return carry

        return run

    for stream in range(2 * mine):
        lax.fori_loop(0, blocks, second_block(stream), 0)
        if rest:
            rest.pop(0)()
        lax.fori_loop(0, col_blocks, second_filter(stream), 0)
    for event in rest:
        event()

    def out_copy(b, incoming):
        return remote(
            stage.at[b],
            out_ref.at[(other if incoming else j) * mine + b],
            out_send.at[b],
            out_recv.at[b],
            (other, q),
        )

    pairs_in(1)
    for b in range(mine):
        for h in (other, j):
            half = pl.ds(pl.multiple_of(h * width, 128), width)
            taken = d1_buf[2 * b : 2 * b + 2].reshape(2 * runs, channels)
            product = jnp.dot(taken, weights[1, h], preferred_element_type=jnp.float32)
            level_rows = x1_buf[2 * b : 2 * b + 2, margin : margin + runs, half]
            level_rows = level_rows.reshape(2 * runs, width)
            mixed = (level_rows.astype(jnp.float32) + product).astype(jnp.bfloat16)
            pooled = jnp.maximum(mixed[:runs], mixed[runs:])
            if h is other:
                stage[b] = pooled
                out_copy(b, False).start()
            else:
                out_ref[j * mine + b] = pooled

    for b in range(mine):
        out_copy(b, True).wait_recv()
        out_copy(b, False).wait_send()
    for copy in swap:
        copy.wait_send()
    to_right.wait_send()
    to_left.wait_send()
    share.wait_send()
    sends_done(0)
    sends_done(1)


def fused(bases, stem_weight, gains, depth_taps, point_weight):
    n_seq = lax.axis_size("seq")
    sequences, width_rows = bases.shape
    channels = stem_weight.shape[2]
    runs = width_rows // GROUP
    rows = runs + BLOCK
    streams = sequences // 2 * GROUP
    half = channels // 2
    n_z = n_seq // 4
    slots = 4 * n_z - 1
    vmem = pl.BlockSpec(memory_space=pltpu.VMEM)
    dma = pltpu.SemaphoreType.DMA
    return pl.pallas_call(
        functools.partial(encoder_kernel, n_seq),
        out_shape=jax.ShapeDtypeStruct((sequences, runs, half), jnp.bfloat16),
        in_specs=[vmem] * 5,
        out_specs=vmem,
        scratch_shapes=[
            pltpu.VMEM((sequences, width_rows + 256), jnp.int32),
            pltpu.VMEM((2, 8, channels), jnp.float32),
            pltpu.VMEM((128, channels), jnp.float32),
            pltpu.VMEM((128, channels), jnp.bfloat16),
            pltpu.VMEM((128, width_rows + 128), jnp.float32),
            pltpu.VMEM((width_rows + 128, 128), jnp.float32),
            pltpu.VMEM((streams, rows, 128), jnp.bfloat16),
            pltpu.VMEM((streams, rows, channels), jnp.bfloat16),
            pltpu.VMEM((streams, rows, channels), jnp.float32),
            pltpu.VMEM((streams, rows, channels), jnp.bfloat16),
            pltpu.VMEM((streams // 2, rows, channels), jnp.bfloat16),
            pltpu.VMEM((streams // 2, runs, channels), jnp.bfloat16),
            pltpu.VMEM((2, 2, channels, half), jnp.bfloat16),
            pltpu.VMEM((sequences // 2, runs, half), jnp.bfloat16),
            dma((2, slots)),
            dma((2, slots)),
            dma((2, slots)),
            dma((2, slots)),
            dma((5,)),
            dma((5,)),
            dma((3,)),
            dma((sequences // 2,)),
            dma((sequences // 2,)),
        ],
        compiler_params=pltpu.CompilerParams(
            collective_id=0, has_side_effects=True, vmem_limit_bytes=56 * 1024 * 1024
        ),
    )(bases, stem_weight, gains, depth_taps, point_weight)


def chosen(bases, stem_weight, gains, depth_taps, point_weight):
    n_seq = lax.axis_size("seq")
    taps, kinds, channels = stem_weight.shape
    fits = lax.axis_size("section") == 2 and n_seq % 4 == 0 and depth_taps.shape[1] == 5
    fits = fits and bases.shape[1] == GROUP * 128 and bases.shape[0] % 2 == 0
    fits = fits and channels % 256 == 0 and point_weight.shape[1] % BLOCK == 0
    fits = fits and kinds == 4 and taps * kinds <= 128
    run = fused if fits else shards
    return run(bases, stem_weight, gains, depth_taps, point_weight)


def solution(mesh):
    return jax.shard_map(
        chosen,
        mesh=mesh,
        in_specs=(
            P(None, "seq"),
            P(),
            P("section", None),
            P("section", None, None),
            P("section", "seq", None),
        ),
        out_specs=P(None, "seq", "section"),
        check_vma=False,
    )
```
